1024 devices in a mesh: dp: 128 (over x_lo, z, core), fsdp: 8 (over y, x_hi).
Axes of the slice: x: 4 (x_hi: 2, x_lo: 2; x = x_hi * 2 + x_lo), y: 4, z: 32, core: 2. Of those that a mesh axis runs over, the one named last changes fastest.
Arguments:
- activations: bfloat16 [32768, 4096], P('dp', 'fsdp'), may hold values from -6 to 6
- proj_basis: bfloat16 [4096, 512], replicated, may hold values from -0.09375 to 0.09375
- out_grad: bfloat16 [32768, 6144], P('dp', 'fsdp')
- master_weight: float32 [4096, 6144], P('dp', 'fsdp'), may hold values from -4 to 4
- first_moment: float32 [512, 6144], P('dp', 'fsdp'), may hold values from -3 to 3
- second_moment: float32 [512, 6144], P('dp', 'fsdp'), may hold values from 0.0001 to 0.01
Outputs:
- new_weight: float32 [4096, 6144], P('dp')
- new_first: float32 [512, 6144], P('dp', 'fsdp')
- new_second: float32 [512, 6144], P('dp', 'fsdp')
The draws below stay inside these ranges and needn't reach their ends.
All inputs are finite; a program needn't handle non-finite values.
Results may differ from the reference program's by a relative error of at most 0.0024.
Values may be sent and summed in bfloat16 or wider, within the bound.
No kernel may reach another device: no remote copies, remote signals or barrier semaphores. Data moves between devices by JAX's collectives and lax.ppermute only.
A program may use at most 32 MiB of HBM per device.

```python
import math
import jax
import jax.numpy as jnp
from jax import lax

D = 4096
F = 6144
R = 512
TOKENS = 32768


def draw_out_grad(key, part):
    key = jax.random.fold_in(key, 11)
    scale = 1.0 / math.sqrt(TOKENS)
    values = jax.random.normal(key, (TOKENS, F), jnp.float32)
    return (values * scale).astype(jnp.bfloat16)


def level_of(stream_key, dims, cuts, smallest, high):
    gain, own = 1.0, jax.random.fold_in(stream_key, 6)
    for position, blocks in cuts:
        heights = jnp.exp(jax.random.uniform(jax.random.fold_in(own, position), (blocks,), jnp.float32, smallest / len(cuts), high / len(cuts)))
        gain = gain * jnp.repeat(heights, dims[position] // blocks).reshape([-1 if axis == position else 1 for axis in range(len(dims))])
    return gain


def centred(rng, shape, width, reach, cuts=(), kind=jnp.bfloat16):
    result = width * jax.random.normal(rng, shape, jnp.float32)
    if cuts:
        result = result * level_of(rng, shape, cuts, -0.22, 0.18)
    return jnp.clip(result, -reach, reach).astype(kind)


def setup_inputs(seed: int = 0) -> dict:
    key_list = jax.random.split(jax.random.key(seed), 7)
    activations = centred(key_list[0], (TOKENS, D), 1.0, 6.0, ((0, 128), (1, 8)))
    proj_basis = centred(key_list[1], (D, R), D ** -0.5, 0.09375)
    out_grad = draw_out_grad(jax.random.fold_in(key_list[6], 71), 0)
    master_weight = centred(key_list[3], (D, F), 1.0, 4.0, ((0, 128), (1, 8)), jnp.float32)
    first_moment = centred(key_list[4], (R, F), 0.3, 3.0, ((0, 128), (1, 8)), jnp.float32)
    second_moment = jnp.clip(jnp.exp(math.log(0.01) - 4.6051702 * jax.random.uniform(key_list[5], (R, F), jnp.float32) ** level_of(key_list[5], (R, F), ((0, 128), (1, 8)), -0.2, 0.2)), 0.0001, 0.01)
    return dict(activations=activations, proj_basis=proj_basis, out_grad=out_grad, master_weight=master_weight, first_moment=first_moment, second_moment=second_moment)


beta_one = 0.9
beta_two = 0.999
adam_step = 2
eps_value = 1e-08
step_size = 1.0

def reference(activations, proj_basis, out_grad, master_weight, first_moment, second_moment):
    coords = jnp.dot(activations, proj_basis, preferred_element_type=jnp.float32).astype(jnp.bfloat16)
    grad = lax.dot_general(coords, out_grad, (((0,), (0,)), ((), ())), preferred_element_type=jnp.float32)
    new_first = beta_one * first_moment + (1.0 - beta_one) * grad
    new_second = beta_two * second_moment + (1.0 - beta_two) * grad * grad
    correct_one = 1.0 - beta_one ** adam_step
    correct_two = 1.0 - beta_two ** adam_step
    update = (new_first / correct_one / (jnp.sqrt(new_second / correct_two) + eps_value)).astype(jnp.bfloat16)
    delta = jnp.dot(proj_basis, update, preferred_element_type=jnp.float32)
    new_weight = master_weight - step_size * delta
    return (new_weight, new_first, new_second)
```

```python
import jax
import jax.numpy as jnp
from jax import lax
from jax.sharding import Mesh, PartitionSpec as P

beta_one = 0.9
beta_two = 0.999
adam_step = 2
eps_value = 1e-08
step_size = 1.0

f32 = jnp.float32
bf16 = jnp.bfloat16
DP = ("xl", "zh", "zl", "c")
FS = ("y", "xh")


def swap(x, axis):
    return lax.ppermute(x, axis, [(0, 1), (1, 0)])


def exchange(x, axis):
    return lax.all_to_all(x, axis, 0, 0, tiled=False)


def spread(x, axis, n):
    return exchange(jnp.broadcast_to(x[None], (n,) + x.shape), axis)


def pair_sum(x, axis, kind):
    me = lax.axis_index(axis)
    mine = lax.dynamic_index_in_dim(x, me, 0, keepdims=False)
    other = lax.dynamic_index_in_dim(x, 1 - me, 0, keepdims=False)
    return mine + swap(other.astype(kind), axis).astype(f32)


def pair_gather(x, axis):
    me = lax.axis_index(axis)
    other = swap(x, axis)
    first = jnp.where(me == 0, x, other)
    second = jnp.where(me == 0, other, x)
    return jnp.stack([first, second])


def rank_order(sizes, total):
    xl, zh, zl, c = (sizes[a] for a in DP)
    depth = total // (xl * zh * zl * c)
    new = lax.broadcasted_iota(jnp.int32, (total, total), 1)
    j = new % depth
    rest = new // depth
    izh = rest % zh
    rest = rest // zh
    izl = rest % zl
    rest = rest // zl
    ixl = rest % xl
    ic = rest // xl
    old = (((ixl * zh + izh) * zl + izl) * c + ic) * depth + j
    return (lax.broadcasted_iota(jnp.int32, (total, total), 0) == old).astype(bf16)


def build(sizes):
    xl, zh, zl, c = (sizes[a] for a in DP)
    nf = sizes["y"] * sizes["xh"]

    def body(activations, proj_basis, out_grad, master_weight, first_moment, second_moment):
        tokens, feats = activations.shape
        ranks = proj_basis.shape[1]
        width = out_grad.shape[1]
        depth = first_moment.shape[0]
        height = master_weight.shape[0]
        order = rank_order(sizes, ranks)

        part_basis = lax.dynamic_slice_in_dim(proj_basis, lax.axis_index(FS) * feats, feats, 0)
        part = jnp.dot(activations, part_basis, preferred_element_type=f32)
        part = exchange(part.reshape(nf, tokens // nf, ranks), FS)
        own = jnp.sum(part, axis=0).astype(bf16)
        own = jnp.dot(own, order, preferred_element_type=f32).astype(bf16)
        coords = spread(own, FS, nf).reshape(tokens, ranks)

        grad = lax.dot_general(
            coords, out_grad, (((0,), (0,)), ((), ())), preferred_element_type=f32
        )
        grad = pair_sum(grad.reshape(c, ranks // c, width), "c", f32)
        grad = pair_sum(grad.reshape(xl, ranks // c // xl, width), "xl", bf16)
        grad = exchange(grad.reshape(zl, zh * depth, width).astype(bf16), "zl")
        grad = jnp.sum(grad.astype(f32), axis=0)
        grad = exchange(grad.reshape(zh, depth, width), "zh")
        grad = jnp.sum(grad, axis=0)

        new_first = beta_one * first_moment + (1.0 - beta_one) * grad
        new_second = beta_two * second_moment + (1.0 - beta_two) * grad * grad
        correct_one = 1.0 - beta_one**adam_step
        correct_two = 1.0 - beta_two**adam_step
        update = (
            new_first / correct_one / (jnp.sqrt(new_second / correct_two) + eps_value)
        ).astype(bf16)

        full = spread(update, "zh", zh).reshape(zh * depth, width)
        full = spread(full, "zl", zl).reshape(zl * zh * depth, width)
        full = pair_gather(full, "xl").reshape(ranks // c, width)
        full = pair_gather(full, "c").reshape(ranks, width)

        basis_rows = lax.dynamic_slice_in_dim(proj_basis, lax.axis_index(DP) * height, height, 0)
        basis_rows = jnp.dot(basis_rows, order, preferred_element_type=f32).astype(bf16)
        delta = jnp.dot(basis_rows, full, preferred_element_type=f32)
        fresh = master_weight - step_size * delta
        new_weight = spread(fresh, FS, nf)
        new_weight = jnp.concatenate([new_weight[i] for i in range(nf)], axis=1)
        return (new_weight, new_first, new_second)

    return body


def split(mesh):
    names = ("xl", "zh", "zl", "c", "y", "xh")
    return Mesh(mesh.devices.reshape(2, 8, 4, 2, 4, 2), names)


def run_on(fine):
    sizes = dict(fine.shape)
    in_specs = (P(DP, FS), P(), P(DP, FS), P(DP, FS), P(DP, FS), P(DP, FS))
    out_specs = (P(DP, None), P(DP, FS), P(DP, FS))
    return jax.shard_map(
        build(sizes), mesh=fine, in_specs=in_specs, out_specs=out_specs, check_vma=False
    )


def solution(mesh):
    return run_on(split(mesh))
```

```python
import jax
import jax.numpy as jnp
from jax import lax
from jax.sharding import Mesh, PartitionSpec as P

beta_one = 0.9
beta_two = 0.999
adam_step = 2
eps_value = 1e-08
step_size = 1.0

f32 = jnp.float32
bf16 = jnp.bfloat16
DP = ("xl", "zh", "zl", "c")
FS = ("y", "xh")


def swap(x, axis):
    return lax.ppermute(x, axis, [(0, 1), (1, 0)])


def exchange(x, axis):
    return lax.all_to_all(x, axis, 0, 0, tiled=False)


def spread(x, axis, n):
    return exchange(jnp.broadcast_to(x[None], (n,) + x.shape), axis)


def rank_order(sizes, total):
    xl, zh, zl, c = (sizes[a] for a in DP)
    depth = total // (xl * zh * zl * c)
    new = lax.broadcasted_iota(jnp.int32, (total, total), 1)
    j = new % depth
    rest = new // depth
    izh = rest % zh
    rest = rest // zh
    izl = rest % zl
    rest = rest // zl
    ixl = rest % xl
    ic = rest // xl
    old = (((ixl * zh + izh) * zl + izl) * c + ic) * depth + j
    return (lax.broadcasted_iota(jnp.int32, (total, total), 0) == old).astype(bf16)


def build(sizes):
    xl, zh, zl, c = (sizes[a] for a in DP)
    nf = sizes["y"] * sizes["xh"]

    def body(activations, proj_basis, out_grad, master_weight, first_moment, second_moment):
        tokens, feats = activations.shape
        ranks = proj_basis.shape[1]
        width = out_grad.shape[1]
        depth = first_moment.shape[0]
        height = master_weight.shape[0]
        order = rank_order(sizes, ranks)

        acts = exchange(activations.reshape(nf, tokens // nf, feats), FS)
        own = lax.dot_general(
            acts,
            proj_basis.reshape(nf, feats, ranks),
            (((0, 2), (0, 1)), ((), ())),
            preferred_element_type=f32,
        ).astype(bf16)
        own = jnp.dot(own, order, preferred_element_type=f32).astype(bf16)
        own = own.reshape(tokens // nf, c * xl, ranks // (c * xl)).swapaxes(0, 1)
        own = jnp.broadcast_to(own[:, None], (c * xl, nf) + own.shape[1:])
        own = own.reshape((c * xl * nf,) + own.shape[2:])
        coords = exchange(own, ("c", "xl", "y", "xh"))
        coords = coords.reshape(c * xl, tokens, ranks // (c * xl))

        me = lax.axis_index("c") * xl + lax.axis_index("xl")
        og_x = swap(out_grad, "xl")
        og_c = swap(out_grad, "c")
        og_xc = swap(og_x, "c")
        blocks = ((me, out_grad), (me ^ 2, og_c), (me ^ 1, og_x), (me ^ 3, og_xc))
        grad = sum(
            lax.dot_general(
                lax.dynamic_index_in_dim(coords, i, 0, keepdims=False),
                og,
                (((0,), (0,)), ((), ())),
                preferred_element_type=f32,
            )
            for i, og in blocks
        )
        grad = exchange(grad.reshape(zl, zh * depth, width).astype(bf16), "zl")
        grad = jnp.sum(grad.astype(f32), axis=0)
        grad = exchange(grad.reshape(zh, depth, width).astype(bf16), "zh")
        grad = jnp.sum(grad.astype(f32), axis=0)

        new_first = beta_one * first_moment + (1.0 - beta_one) * grad
        new_second = beta_two * second_moment + (1.0 - beta_two) * grad * grad
        correct_one = 1.0 - beta_one**adam_step
        correct_two = 1.0 - beta_two**adam_step
        update = (
            new_first / correct_one / (jnp.sqrt(new_second / correct_two) + eps_value)
        ).astype(bf16)

        full = spread(update, "zh", zh).reshape(zh * depth, width)
        full = spread(full, ("xl", "zl"), xl * zl).reshape(ranks // c, width)
        other = swap(full, "c")

        basis_rows = lax.dynamic_slice_in_dim(proj_basis, lax.axis_index(DP) * height, height, 0)
        basis_rows = jnp.dot(basis_rows, order, preferred_element_type=f32).astype(bf16)
        basis_rows = basis_rows.reshape(height, c, ranks // c).swapaxes(0, 1)
        core = lax.axis_index("c")
        delta = jnp.dot(
            lax.dynamic_index_in_dim(basis_rows, core, 0, keepdims=False),
            full,
            preferred_element_type=f32,
        )
        delta = delta + jnp.dot(
            lax.dynamic_index_in_dim(basis_rows, 1 - core, 0, keepdims=False),
            other,
            preferred_element_type=f32,
        )
        fresh = master_weight - step_size * delta
        new_weight = spread(fresh, FS, nf)
        new_weight = jnp.concatenate([new_weight[i] for i in range(nf)], axis=1)
        return (new_weight, new_first, new_second)

    return body


def split(mesh):
    names = ("xl", "zh", "zl", "c", "y", "xh")
    return Mesh(mesh.devices.reshape(2, 8, 4, 2, 4, 2), names)


def run_on(fine):
    sizes = dict(fine.shape)
    in_specs = (P(DP, FS), P(), P(DP, FS), P(DP, FS), P(DP, FS), P(DP, FS))
    out_specs = (P(DP, None), P(DP, FS), P(DP, FS))
    return jax.shard_map(
        build(sizes), mesh=fine, in_specs=in_specs, out_specs=out_specs, check_vma=False
    )


def solution(mesh):
    return run_on(split(mesh))
```

```python
import jax
import jax.numpy as jnp
from jax import lax
from jax.sharding import Mesh, PartitionSpec as P

beta_one = 0.9
beta_two = 0.999
adam_step = 2
eps_value = 1e-08
step_size = 1.0

f32 = jnp.float32
bf16 = jnp.bfloat16
DP = ("xl", "zh", "zl", "c")
FS = ("y", "xh")


def swap(x, axis):
    return lax.ppermute(x, axis, [(0, 1), (1, 0)])


def exchange(x, axis):
    return lax.all_to_all(x, axis, 0, 0, tiled=False)


def spread(x, axis, n):
    return exchange(jnp.broadcast_to(x[None], (n,) + x.shape), axis)


def double(x, axis, gap, pieces=1):
    pairs = [(i, i ^ gap) for i in range(lax.axis_size(axis))]
    got = [lax.ppermute(part, axis, pairs) for part in jnp.split(x, pieces)]
    return jnp.concatenate([x] + got)


def rank_order(sizes, total):
    xl, zh, zl, c = (sizes[a] for a in DP)
    depth = total // (xl * zh * zl * c)
    new = lax.broadcasted_iota(jnp.int32, (total, total), 1)
    j = new % depth
    rest = new // depth
    izh = rest % zh
    rest = rest // zh
    izl = rest % zl
    rest = rest // zl
    ixl = rest % xl
    ic = rest // xl
    old = (((ixl * zh + izh) * zl + izl) * c + ic) * depth + j
    return (lax.broadcasted_iota(jnp.int32, (total, total), 0) == old).astype(bf16)


def build(sizes):
    xl, zh, zl, c = (sizes[a] for a in DP)
    nf = sizes["y"] * sizes["xh"]

    def body(activations, proj_basis, out_grad, master_weight, first_moment, second_moment):
        tokens, feats = activations.shape
        ranks = proj_basis.shape[1]
        width = out_grad.shape[1]
        depth = first_moment.shape[0]
        height = master_weight.shape[0]
        order = rank_order(sizes, ranks)

        basis = jnp.dot(proj_basis, order, preferred_element_type=f32).astype(bf16)

        acts = exchange(activations.reshape(nf, tokens // nf, feats), FS)
        own = lax.dot_general(
            acts,
            basis.reshape(nf, feats, ranks),
            (((0, 2), (0, 1)), ((), ())),
            preferred_element_type=f32,
        ).astype(bf16)
        own = own.reshape(tokens // nf, c * xl, ranks // (c * xl)).swapaxes(0, 1)
        own = jnp.broadcast_to(own[:, None], (c * xl, nf) + own.shape[1:])
        own = own.reshape((c * xl * nf,) + own.shape[2:])
        coords = exchange(own, ("c", "xl", "y", "xh"))
        coords = coords.reshape(c * xl, tokens, ranks // (c * xl))

        me = lax.axis_index("c") * xl + lax.axis_index("xl")
        og_x = swap(out_grad, "xl")
        og_c = swap(out_grad, "c")
        og_xc = swap(og_x, "c")
        blocks = ((me, out_grad), (me ^ 2, og_c), (me ^ 1, og_x), (me ^ 3, og_xc))
        grad = sum(
            lax.dot_general(
                lax.dynamic_index_in_dim(coords, i, 0, keepdims=False),
                og,
                (((0,), (0,)), ((), ())),
                preferred_element_type=f32,
            )
            for i, og in blocks
        )
        grad, weights = lax.optimization_barrier((grad.astype(bf16), master_weight[None]))
        grad = exchange(grad.reshape(zl, zh * depth, width), "zl")
        weights = double(weights, "y", 1)
        grad, weights = lax.optimization_barrier((grad, weights))
        grad = jnp.sum(grad.astype(f32), axis=0).astype(bf16)
        grad, weights = lax.optimization_barrier((grad, weights))
        grad = exchange(grad.reshape(zh, depth, width), "zh")
        weights = double(weights, "xh", 1)
        grad, weights = lax.optimization_barrier((grad, weights))
        grad = jnp.sum(grad.astype(f32), axis=0)

        new_first = beta_one * first_moment + (1.0 - beta_one) * grad
        new_second = beta_two * second_moment + (1.0 - beta_two) * grad * grad
        correct_one = 1.0 - beta_one**adam_step
        correct_two = 1.0 - beta_two**adam_step
        update = (
            new_first / correct_one / (jnp.sqrt(new_second / correct_two) + eps_value)
        ).astype(bf16)

        full = jnp.broadcast_to(update[None], (zh,) + update.shape)
        full, weights = lax.optimization_barrier((full, weights))
        full = exchange(full, "zh")
        weights = double(weights, "y", 2, 2)
        full, weights = lax.optimization_barrier((full, weights))
        full = spread(full.reshape(zh * depth, width), ("xl", "zl"), xl * zl)
        full = full.reshape(ranks // c, width)
        other = swap(full, "c")

        basis_rows = lax.dynamic_slice_in_dim(basis, lax.axis_index(DP) * height, height, 0)
        basis_rows = basis_rows.reshape(height, c, ranks // c).swapaxes(0, 1)
        core = lax.axis_index("c")
        delta = jnp.dot(
            lax.dynamic_index_in_dim(basis_rows, core, 0, keepdims=False),
            full,
            preferred_element_type=f32,
        )
        delta = delta + jnp.dot(
            lax.dynamic_index_in_dim(basis_rows, 1 - core, 0, keepdims=False),
            other,
            preferred_element_type=f32,
        )
        deltas = spread(delta.astype(bf16), FS, nf)
        place = lax.axis_index(FS)

        def block(other):
            m = place ^ other
            return (m & 4) | ((m & 1) << 1) | ((m >> 1) & 1)

        new_weight = jnp.concatenate(
            [
                lax.dynamic_index_in_dim(weights, block(i), 0, keepdims=False)
                - step_size * deltas[i].astype(f32)
                for i in range(nf)
            ],
            axis=1,
        )
        return (new_weight, new_first, new_second)

    return body


def split(mesh):
    names = ("xl", "zh", "zl", "c", "y", "xh")
    return Mesh(mesh.devices.reshape(2, 8, 4, 2, 4, 2), names)


def run_on(fine):
    sizes = dict(fine.shape)
    in_specs = (P(DP, FS), P(), P(DP, FS), P(DP, FS), P(DP, FS), P(DP, FS))
    out_specs = (P(DP, None), P(DP, FS), P(DP, FS))
    return jax.shard_map(
        build(sizes), mesh=fine, in_specs=in_specs, out_specs=out_specs, check_vma=False
    )


def solution(mesh):
    return run_on(split(mesh))
```

```python
import jax
import jax.numpy as jnp
from jax import lax
from jax.experimental import pallas as pl
from jax.experimental.pallas import tpu as pltpu
from jax.sharding import Mesh, PartitionSpec as P

beta_one = 0.9
beta_two = 0.999
adam_step = 2
eps_value = 1e-08
step_size = 1.0

f32 = jnp.float32
bf16 = jnp.bfloat16
DP = ("xl", "zh", "zl", "c")
FS = ("y", "xh")


def swap(x, axis):
    return lax.ppermute(x, axis, [(0, 1), (1, 0)])


def exchange(x, axis):
    return lax.all_to_all(x, axis, 0, 0, tiled=False)


def spread(x, axis, n):
    return exchange(jnp.broadcast_to(x[None], (n,) + x.shape), axis)


def rank_order(sizes, total):
    zh, zl, c = (sizes[a] for a in ("zh", "zl", "c"))
    depth = total // (zh * zl * c)
    new = lax.broadcasted_iota(jnp.int32, (1, total), 1)
    j = new % depth
    rest = new // depth
    izh = rest % zh
    rest = rest // zh
    old = ((izh * zl + rest % zl) * c + rest // zl) * depth + j
    return (lax.broadcasted_iota(jnp.int32, (total, total), 0) == old).astype(bf16)


def coords_kernel(acts_ref, basis_ref, order_ref, out_ref, total):
    step = pl.program_id(0)
    part = jnp.dot(acts_ref[0], basis_ref[0], preferred_element_type=f32)

    @pl.when(step == 0)
    def _():
        total[...] = part

    @pl.when(step > 0)
    def _():
        total[...] += part

    @pl.when(step == pl.num_programs(0) - 1)
    def _():
        own = total[...].astype(bf16)
        block = order_ref.shape[0]
        groups, copies, _, wide = out_ref.shape
        per = block // wide
        for x in range(groups // per):
            half = own[:, x * block : (x + 1) * block]
            half = jnp.dot(half, order_ref[...], preferred_element_type=f32).astype(bf16)
            for k in range(per):
                piece = half[:, k * wide : (k + 1) * wide]
                for i in range(copies):
                    out_ref[x * per + k, i] = piece


def coords_copies(acts, basis, order, groups):
    nf, tokens, feats = acts.shape
    ranks = basis.shape[-1]
    return pl.pallas_call(
        coords_kernel,
        grid=(nf,),
        in_specs=[
            pl.BlockSpec((1, tokens, feats), lambda i: (i, 0, 0)),
            pl.BlockSpec((1, feats, ranks), lambda i: (i, 0, 0)),
            pl.BlockSpec(order.shape, lambda i: (0, 0)),
        ],
        out_specs=pl.BlockSpec((groups, nf, tokens, ranks // groups), lambda i: (0, 0, 0, 0)),
        out_shape=jax.ShapeDtypeStruct((groups, nf, tokens, ranks // groups), bf16),
        scratch_shapes=[pltpu.VMEM((tokens, ranks), f32)],
        cost_estimate=pl.CostEstimate(
            flops=2 * nf * tokens * feats * ranks,
            bytes_accessed=2 * nf * feats * (tokens + ranks),
            transcendentals=0,
        ),
        compiler_params=pltpu.CompilerParams(vmem_limit_bytes=52 * 1024 * 1024),
    )(acts, basis, order)


def build(sizes):
    xl, zh, zl, c = (sizes[a] for a in DP)
    nf = sizes["y"] * sizes["xh"]

    def body(activations, proj_basis, out_grad, master_weight, first_moment, second_moment):
        tokens, feats = activations.shape
        ranks = proj_basis.shape[1]
        width = out_grad.shape[1]
        depth = first_moment.shape[0]
        height = master_weight.shape[0]
        order = rank_order(sizes, ranks // xl)

        acts = exchange(activations.reshape(nf, tokens // nf, feats), FS)
        own = coords_copies(acts, proj_basis.reshape(nf, feats, ranks), order, xl * c)
        own = own.reshape((xl * c * nf,) + own.shape[2:])
        coords = exchange(own, ("xl", "c", "y", "xh"))
        coords = coords.reshape(xl * c, tokens, ranks // (xl * c))

        me = lax.axis_index("xl") * c + lax.axis_index("c")
        og_x = swap(out_grad, "xl")
        og_c = swap(out_grad, "c")
        og_xc = swap(og_x, "c")
        blocks = ((me, out_grad), (me ^ 1, og_c), (me ^ 2, og_x), (me ^ 3, og_xc))
        grad = sum(
            lax.dot_general(
                lax.dynamic_index_in_dim(coords, i, 0, keepdims=False),
                og,
                (((0,), (0,)), ((), ())),
                preferred_element_type=f32,
            )
            for i, og in blocks
        )
        grad = exchange(grad.reshape(zl, zh * depth, width).astype(bf16), "zl")
        grad = jnp.sum(grad.astype(f32), axis=0)
        grad = exchange(grad.reshape(zh, depth, width).astype(bf16), "zh")

        rows = lax.dynamic_slice_in_dim(proj_basis, lax.axis_index(DP) * height, height, 0)
        block = ranks // xl
        rows = [
            jnp.dot(
                rows[:, i * block : (i + 1) * block], order, preferred_element_type=f32
            ).astype(bf16)
            for i in range(xl)
        ]
        piece = block // c
        basis_rows = jnp.stack(
            [
                jnp.concatenate([r[:, k * piece : (k + 1) * piece] for r in rows], axis=1)
                for k in range(c)
            ]
        )
        grad, basis_rows = lax.optimization_barrier((grad, basis_rows))
        grad = jnp.sum(grad.astype(f32), axis=0)

        new_first = beta_one * first_moment + (1.0 - beta_one) * grad
        new_second = beta_two * second_moment + (1.0 - beta_two) * grad * grad
        correct_one = 1.0 - beta_one**adam_step
        correct_two = 1.0 - beta_two**adam_step
        update = (
            new_first / correct_one / (jnp.sqrt(new_second / correct_two) + eps_value)
        ).astype(bf16)

        full = spread(update, "zh", zh).reshape(zh * depth, width)
        full = spread(full, ("xl", "zl"), xl * zl).reshape(ranks // c, width)
        other = swap(full, "c")

        core = lax.axis_index("c")
        delta = jnp.dot(
            lax.dynamic_index_in_dim(basis_rows, core, 0, keepdims=False),
            full,
            preferred_element_type=f32,
        )
        delta = delta + jnp.dot(
            lax.dynamic_index_in_dim(basis_rows, 1 - core, 0, keepdims=False),
            other,
            preferred_element_type=f32,
        )
        fresh = master_weight - step_size * delta
        new_weight = spread(fresh, FS, nf)
        new_weight = jnp.concatenate([new_weight[i] for i in range(nf)], axis=1)
        return (new_weight, new_first, new_second)

    return body


def split(mesh):
    names = ("xl", "zh", "zl", "c", "y", "xh")
    return Mesh(mesh.devices.reshape(2, 8, 4, 2, 4, 2), names)


def run_on(fine):
    sizes = dict(fine.shape)
    in_specs = (P(DP, FS), P(), P(DP, FS), P(DP, FS), P(DP, FS), P(DP, FS))
    out_specs = (P(DP, None), P(DP, FS), P(DP, FS))
    return jax.shard_map(
        build(sizes), mesh=fine, in_specs=in_specs, out_specs=out_specs, check_vma=False
    )


def solution(mesh):
    return run_on(split(mesh))
```

```python
import jax
import jax.numpy as jnp
from jax import lax
from jax.sharding import Mesh, PartitionSpec as P

beta_one = 0.9
beta_two = 0.999
adam_step = 2
eps_value = 1e-08
step_size = 1.0

f32 = jnp.float32
bf16 = jnp.bfloat16
DP = ("xl", "zh", "zl", "c")
FS = ("y", "xh")


def swap(x, axis):
    return lax.ppermute(x, axis, [(0, 1), (1, 0)])


def exchange(x, axis):
    return lax.all_to_all(x, axis, 0, 0, tiled=False)


def spread(x, axis, n):
    return exchange(jnp.broadcast_to(x[None], (n,) + x.shape), axis)


def rank_order(sizes, total):
    zh, zl = sizes["zh"], sizes["zl"]
    unit = total // (zh * zl)
    new = lax.broadcasted_iota(jnp.int32, (1, total), 1)
    rest = new // unit
    old = ((rest % zh) * zl + rest // zh) * unit + new % unit
    return (lax.broadcasted_iota(jnp.int32, (total, total), 0) == old).astype(bf16)


def pick(x, i):
    return lax.dynamic_index_in_dim(x, i, 0, keepdims=False)


def build(sizes):
    xl, zh, zl, c = (sizes[a] for a in DP)
    nf = sizes["y"] * sizes["xh"]

    def body(activations, proj_basis, out_grad, master_weight, first_moment, second_moment):
        tokens, feats = activations.shape
        ranks = proj_basis.shape[1]
        width = out_grad.shape[1]
        depth = first_moment.shape[0]
        height = master_weight.shape[0]
        unit = c * depth
        half = width // c
        block = ranks // xl
        core, side = lax.axis_index("c"), lax.axis_index("xl")

        acts = exchange(activations.reshape(nf, tokens // nf, feats), FS)

        order = rank_order(sizes, block)
        rows = lax.dynamic_slice_in_dim(
            proj_basis, (lax.axis_index(DP) - core) * height, c * height, 0
        )
        rows = jnp.concatenate(
            [
                jnp.dot(
                    rows[:, i * block : (i + 1) * block], order, preferred_element_type=f32
                ).astype(bf16)
                for i in range(xl)
            ],
            axis=1,
        )
        acts, rows = lax.optimization_barrier((acts, rows))

        own = lax.dot_general(
            acts,
            proj_basis.reshape(nf, feats, ranks),
            (((0, 2), (0, 1)), ((), ())),
            preferred_element_type=f32,
        ).astype(bf16)
        own = jnp.stack([own[:, i * block : (i + 1) * block] for i in range(xl)])
        own = jnp.broadcast_to(own[:, None], (xl, nf) + own.shape[1:])
        coords = exchange(own.reshape(xl * nf, tokens // nf, block), ("xl", "y", "xh"))
        coords = coords.reshape(xl, tokens, block)

        def halves(x):
            return jnp.stack([x[:, i * half : (i + 1) * half] for i in range(c)])

        state = halves(jnp.concatenate([master_weight, first_moment, second_moment]))
        mine = pick(state, core)
        theirs = swap(pick(state, 1 - core), "c")
        both = jnp.stack([jnp.where(core == 0, mine, theirs), jnp.where(core == 0, theirs, mine)])
        weight_rows = both[:, :height]
        first = both[:, height : height + depth].reshape(unit, half)
        second = both[:, height + depth :].reshape(unit, half)

        grad = sum(
            lax.dot_general(pick(coords, i), og, (((0,), (0,)), ((), ())), preferred_element_type=f32)
            for i, og in ((side, out_grad), (1 - side, swap(out_grad, "xl")))
        )
        grad = grad.astype(bf16).reshape(zh, zl, unit, c, half).transpose(3, 1, 0, 2, 4)
        grad = exchange(grad.reshape(c * zl, zh * unit, half), ("c", "zl"))
        grad = jnp.sum(grad.astype(f32), axis=0)
        grad = exchange(grad.reshape(zh, unit, half).astype(bf16), "zh")
        grad = jnp.sum(grad.astype(f32), axis=0)

        correct_one = 1.0 - beta_one**adam_step
        correct_two = 1.0 - beta_two**adam_step

        def moments(first, second, grad):
            new_first = beta_one * first + (1.0 - beta_one) * grad
            new_second = beta_two * second + (1.0 - beta_two) * grad * grad
            return new_first, new_second

        new_first, new_second = moments(first, second, grad)
        update = (
            new_first / correct_one / (jnp.sqrt(new_second / correct_two) + eps_value)
        ).astype(bf16)

        full = spread(update, "zh", zh).reshape(zh * unit, half)
        full = spread(full, ("xl", "zl"), xl * zl).reshape(ranks, half)

        parts = grad.reshape(c, depth, half)
        kept = pick(parts, core)
        got = swap(pick(parts, 1 - core), "c")
        grad = jnp.concatenate(
            [jnp.where(core == 0, kept, got), jnp.where(core == 0, got, kept)], axis=1
        )
        new_first, new_second = moments(first_moment, second_moment, grad)

        delta = jnp.dot(rows, full, preferred_element_type=f32)
        fresh = weight_rows - step_size * delta.reshape(c, height, half)
        fresh = jnp.broadcast_to(fresh[None], (nf,) + fresh.shape)
        new_weight = exchange(fresh.reshape(nf * c, height, half), ("y", "xh", "c"))
        new_weight = jnp.concatenate([new_weight[i] for i in range(nf * c)], axis=1)
        return (new_weight, new_first, new_second)

    return body


def split(mesh):
    names = ("xl", "zh", "zl", "c", "y", "xh")
    return Mesh(mesh.devices.reshape(2, 8, 4, 2, 4, 2), names)


def run_on(fine):
    sizes = dict(fine.shape)
    in_specs = (P(DP, FS), P(), P(DP, FS), P(DP, FS), P(DP, FS), P(DP, FS))
    out_specs = (P(DP, None), P(DP, FS), P(DP, FS))
    return jax.shard_map(
        build(sizes), mesh=fine, in_specs=in_specs, out_specs=out_specs, check_vma=False
    )


def solution(mesh):
    return run_on(split(mesh))
```

```python
import jax
import jax.numpy as jnp
from jax import lax
from jax.sharding import Mesh, PartitionSpec as P

beta_one = 0.9
beta_two = 0.999
adam_step = 2
eps_value = 1e-08
step_size = 1.0

f32 = jnp.float32
bf16 = jnp.bfloat16
DP = ("xl", "zh", "zl", "c")
FS = ("y", "xh")


def swap(x, axis):
    return lax.ppermute(x, axis, [(0, 1), (1, 0)])


def exchange(x, axis):
    return lax.all_to_all(x, axis, 0, 0, tiled=False)


def spread(x, axis, n):
    return exchange(jnp.broadcast_to(x[None], (n,) + x.shape), axis)


def rank_order(sizes, total):
    xl, zh, zl, c = (sizes[a] for a in DP)
    depth = total // (xl * zh * zl * c)
    new = lax.broadcasted_iota(jnp.int32, (total, total), 1)
    j = new % depth
    rest = new // depth
    izh = rest % zh
    rest = rest // zh
    izl = rest % zl
    rest = rest // zl
    ixl = rest % xl
    ic = rest // xl
    old = (((ixl * zh + izh) * zl + izl) * c + ic) * depth + j
    return (lax.broadcasted_iota(jnp.int32, (total, total), 0) == old).astype(bf16)


def build(sizes):
    xl, zh, zl, c = (sizes[a] for a in DP)
    nf = sizes["y"] * sizes["xh"]

    def body(activations, proj_basis, out_grad, master_weight, first_moment, second_moment):
        tokens, feats = activations.shape
        ranks = proj_basis.shape[1]
        width = out_grad.shape[1]
        depth = first_moment.shape[0]
        height = master_weight.shape[0]
        order = rank_order(sizes, ranks)

        acts = exchange(activations.reshape(nf, tokens // nf, feats), FS)
        own = lax.dot_general(
            acts,
            proj_basis.reshape(nf, feats, ranks),
            (((0, 2), (0, 1)), ((), ())),
            preferred_element_type=f32,
        ).astype(bf16)
        own = jnp.dot(own, order, preferred_element_type=f32).astype(bf16)
        own = own.reshape(tokens // nf, c * xl, ranks // (c * xl)).swapaxes(0, 1)
        own = jnp.broadcast_to(own[:, None], (c * xl, nf) + own.shape[1:])
        own = own.reshape((c * xl * nf,) + own.shape[2:])
        coords = exchange(own, ("c", "xl", "y", "xh"))
        coords = coords.reshape(c * xl, tokens, ranks // (c * xl))

        me = lax.axis_index("c") * xl + lax.axis_index("xl")
        og_x = swap(out_grad, "xl")
        og_c = swap(out_grad, "c")
        og_xc = swap(og_x, "c")
        blocks = ((me, out_grad), (me ^ 2, og_c), (me ^ 1, og_x), (me ^ 3, og_xc))
        grad = sum(
            lax.dot_general(
                lax.dynamic_index_in_dim(coords, i, 0, keepdims=False),
                og,
                (((0,), (0,)), ((), ())),
                preferred_element_type=f32,
            )
            for i, og in blocks
        )
        grad, weight = lax.optimization_barrier((grad.astype(bf16), master_weight))
        weight = jnp.concatenate([weight, weight[: height // 2]])
        weights = lax.all_gather(weight, FS, axis=0, tiled=False)
        grad = exchange(grad.reshape(zl, zh * depth, width), "zl")
        grad = jnp.sum(grad.astype(f32), axis=0)
        grad = exchange(grad.reshape(zh, depth, width).astype(bf16), "zh")
        grad = jnp.sum(grad.astype(f32), axis=0)

        new_first = beta_one * first_moment + (1.0 - beta_one) * grad
        new_second = beta_two * second_moment + (1.0 - beta_two) * grad * grad
        correct_one = 1.0 - beta_one**adam_step
        correct_two = 1.0 - beta_two**adam_step
        update = (
            new_first / correct_one / (jnp.sqrt(new_second / correct_two) + eps_value)
        ).astype(bf16)

        full = spread(update, "zh", zh)
        full, weights = lax.optimization_barrier((full, weights))
        full = full.reshape(zh * depth, width)
        full = spread(full, ("xl", "zl"), xl * zl).reshape(ranks // c, width)
        other = swap(full, "c")

        basis_rows = lax.dynamic_slice_in_dim(proj_basis, lax.axis_index(DP) * height, height, 0)
        basis_rows = jnp.dot(basis_rows, order, preferred_element_type=f32).astype(bf16)
        basis_rows = basis_rows.reshape(height, c, ranks // c).swapaxes(0, 1)
        core = lax.axis_index("c")
        delta = jnp.dot(
            lax.dynamic_index_in_dim(basis_rows, core, 0, keepdims=False),
            full,
            preferred_element_type=f32,
        )
        delta = delta + jnp.dot(
            lax.dynamic_index_in_dim(basis_rows, 1 - core, 0, keepdims=False),
            other,
            preferred_element_type=f32,
        )
        deltas = spread(delta.astype(bf16), FS, nf)
        new_weight = jnp.concatenate(
            [weights[i, :height] - step_size * deltas[i].astype(f32) for i in range(nf)], axis=1
        )
        return (new_weight, new_first, new_second)

    return body


def split(mesh):
    names = ("xl", "zh", "zl", "c", "y", "xh")
    return Mesh(mesh.devices.reshape(2, 8, 4, 2, 4, 2), names)


def run_on(fine):
    sizes = dict(fine.shape)
    in_specs = (P(DP, FS), P(), P(DP, FS), P(DP, FS), P(DP, FS), P(DP, FS))
    out_specs = (P(DP, None), P(DP, FS), P(DP, FS))
    return jax.shard_map(
        build(sizes), mesh=fine, in_specs=in_specs, out_specs=out_specs, check_vma=False
    )


def solution(mesh):
    return run_on(split(mesh))
```

```python
import jax
import jax.numpy as jnp
from jax import lax
from jax.sharding import Mesh, PartitionSpec as P

beta_one = 0.9
beta_two = 0.999
adam_step = 2
eps_value = 1e-08
step_size = 1.0

f32 = jnp.float32
bf16 = jnp.bfloat16
DP = ("xl", "zh", "zl", "c")
FS = ("y", "xh")


def swap(x, axis):
    return lax.ppermute(x, axis, [(0, 1), (1, 0)])


def exchange(x, axis):
    return lax.all_to_all(x, axis, 0, 0, tiled=False)


def spread(x, axis, n):
    return exchange(jnp.broadcast_to(x[None], (n,) + x.shape), axis)


def rank_order(sizes, total):
    xl, zh, zl, c = (sizes[a] for a in DP)
    depth = total // (xl * zh * zl * c)
    new = lax.broadcasted_iota(jnp.int32, (total, total), 1)
    j = new % depth
    rest = new // depth
    izh = rest % zh
    rest = rest // zh
    izl = rest % zl
    rest = rest // zl
    ixl = rest % xl
    ic = rest // xl
    old = (((ixl * zh + izh) * zl + izl) * c + ic) * depth + j
    return (lax.broadcasted_iota(jnp.int32, (total, total), 0) == old).astype(bf16)


def build(sizes):
    xl, zh, zl, c = (sizes[a] for a in DP)
    nf = sizes["y"] * sizes["xh"]

    def body(activations, proj_basis, out_grad, master_weight, first_moment, second_moment):
        tokens, feats = activations.shape
        ranks = proj_basis.shape[1]
        width = out_grad.shape[1]
        depth = first_moment.shape[0]
        height = master_weight.shape[0]
        order = rank_order(sizes, ranks)

        acts = exchange(activations.reshape(nf, tokens // nf, feats), FS)
        own = lax.dot_general(
            acts,
            proj_basis.reshape(nf, feats, ranks),
            (((0, 2), (0, 1)), ((), ())),
            preferred_element_type=f32,
        ).astype(bf16)
        own = jnp.dot(own, order, preferred_element_type=f32).astype(bf16)
        own = own.reshape(tokens // nf, c * xl, ranks // (c * xl)).swapaxes(0, 1)
        own = jnp.broadcast_to(own[:, None], (c * xl, nf) + own.shape[1:])
        own = own.reshape((c * xl * nf,) + own.shape[2:])
        coords = exchange(own, ("c", "xl", "y", "xh"))
        coords = coords.reshape(c * xl, tokens, ranks // (c * xl))

        me = lax.axis_index("c") * xl + lax.axis_index("xl")
        og_x = swap(out_grad, "xl")
        og_c = swap(out_grad, "c")
        og_xc = swap(og_x, "c")
        blocks = ((me, out_grad), (me ^ 2, og_c), (me ^ 1, og_x), (me ^ 3, og_xc))
        grad = sum(
            lax.dot_general(
                lax.dynamic_index_in_dim(coords, i, 0, keepdims=False),
                og,
                (((0,), (0,)), ((), ())),
                preferred_element_type=f32,
            )
            for i, og in blocks
        )
        grad = exchange(grad.reshape(zl, zh * depth, width).astype(bf16), "zl")
        grad = jnp.sum(grad.astype(f32), axis=0)
        grad = exchange(grad.reshape(zh, depth, width).astype(bf16), "zh")
        grad = jnp.sum(grad.astype(f32), axis=0)

        new_first = beta_one * first_moment + (1.0 - beta_one) * grad
        new_second = beta_two * second_moment + (1.0 - beta_two) * grad * grad
        correct_one = 1.0 - beta_one**adam_step
        correct_two = 1.0 - beta_two**adam_step
        update = (
            new_first / correct_one / (jnp.sqrt(new_second / correct_two) + eps_value)
        ).astype(bf16)

        full = spread(update, "zh", zh).reshape(zh * depth, width)
        full = spread(full, ("c", "xl", "zl"), c * xl * zl).reshape(ranks, width)

        basis_rows = lax.dynamic_slice_in_dim(proj_basis, lax.axis_index(DP) * height, height, 0)
        basis_rows = jnp.dot(basis_rows, order, preferred_element_type=f32).astype(bf16)
        delta = jnp.dot(basis_rows, full, preferred_element_type=f32)
        fresh = master_weight - step_size * delta
        new_weight = spread(fresh, FS, nf)
        new_weight = jnp.concatenate([new_weight[i] for i in range(nf)], axis=1)
        return (new_weight, new_first, new_second)

    return body


def split(mesh):
    names = ("xl", "zh", "zl", "c", "y", "xh")
    return Mesh(mesh.devices.reshape(2, 8, 4, 2, 4, 2), names)


def run_on(fine):
    sizes = dict(fine.shape)
    in_specs = (P(DP, FS), P(), P(DP, FS), P(DP, FS), P(DP, FS), P(DP, FS))
    out_specs = (P(DP, None), P(DP, FS), P(DP, FS))
    return jax.shard_map(
        build(sizes), mesh=fine, in_specs=in_specs, out_specs=out_specs, check_vma=False
    )


def solution(mesh):
    return run_on(split(mesh))
```

```python
import jax
import jax.numpy as jnp
from jax import lax
from jax.sharding import Mesh, PartitionSpec as P

beta_one = 0.9
beta_two = 0.999
adam_step = 2
eps_value = 1e-08
step_size = 1.0

f32 = jnp.float32
bf16 = jnp.bfloat16
DP = ("xl", "zh", "zl", "c")
FS = ("y", "xh")


def swap(x, axis):
    return lax.ppermute(x, axis, [(0, 1), (1, 0)])


def exchange(x, axis):
    return lax.all_to_all(x, axis, 0, 0, tiled=False)


def spread(x, axis, n):
    return exchange(jnp.broadcast_to(x[None], (n,) + x.shape), axis)


def rank_order(sizes, total):
    xl, zh, zl, c = (sizes[a] for a in DP)
    depth = total // (xl * zh * zl * c)
    new = lax.broadcasted_iota(jnp.int32, (total, total), 1)
    j = new % depth
    rest = new // depth
    izh = rest % zh
    rest = rest // zh
    izl = rest % zl
    rest = rest // zl
    ixl = rest % xl
    ic = rest // xl
    old = (((ixl * zh + izh) * zl + izl) * c + ic) * depth + j
    return (lax.broadcasted_iota(jnp.int32, (total, total), 0) == old).astype(bf16)


def back_order(sizes, total):
    zh, zl = sizes["zh"], sizes["zl"]
    unit = total // (zh * zl)
    new = lax.broadcasted_iota(jnp.int32, (total, total), 1)
    rest = new // unit
    old = ((rest % zh) * zl + rest // zh) * unit + new % unit
    return (lax.broadcasted_iota(jnp.int32, (total, total), 0) == old).astype(bf16)


def pick(x, i):
    return lax.dynamic_index_in_dim(x, i, 0, keepdims=False)


def build(sizes):
    xl, zh, zl, c = (sizes[a] for a in DP)
    nf = sizes["y"] * sizes["xh"]

    def body(activations, proj_basis, out_grad, master_weight, first_moment, second_moment):
        tokens, feats = activations.shape
        ranks = proj_basis.shape[1]
        width = out_grad.shape[1]
        depth = first_moment.shape[0]
        height = master_weight.shape[0]
        order = rank_order(sizes, ranks)

        acts = exchange(activations.reshape(nf, tokens // nf, feats), FS)

        core = lax.axis_index("c")
        half, block = width // c, ranks // xl
        back = back_order(sizes, block)
        rows = lax.dynamic_slice_in_dim(
            proj_basis, (lax.axis_index(DP) - core) * height, c * height, 0
        )
        rows = jnp.concatenate(
            [
                jnp.dot(
                    rows[:, i * block : (i + 1) * block], back, preferred_element_type=f32
                ).astype(bf16)
                for i in range(xl)
            ],
            axis=1,
        )
        acts, rows = lax.optimization_barrier((acts, rows))
        own = lax.dot_general(
            acts,
            proj_basis.reshape(nf, feats, ranks),
            (((0, 2), (0, 1)), ((), ())),
            preferred_element_type=f32,
        ).astype(bf16)
        own = jnp.dot(own, order, preferred_element_type=f32).astype(bf16)
        own = own.reshape(tokens // nf, c * xl, ranks // (c * xl)).swapaxes(0, 1)
        own = jnp.broadcast_to(own[:, None], (c * xl, nf) + own.shape[1:])
        own = own.reshape((c * xl * nf,) + own.shape[2:])
        coords = exchange(own, ("c", "xl", "y", "xh"))
        mine = lax.dynamic_slice_in_dim(master_weight, core * half, half, 1)
        theirs = swap(lax.dynamic_slice_in_dim(master_weight, (1 - core) * half, half, 1), "c")
        coords, theirs = lax.optimization_barrier((coords, theirs))
        coords = coords.reshape(c * xl, tokens, ranks // (c * xl))

        me = lax.axis_index("c") * xl + lax.axis_index("xl")
        og_x = swap(out_grad, "xl")
        og_c = swap(out_grad, "c")
        og_xc = swap(og_x, "c")
        blocks = ((me, out_grad), (me ^ 2, og_c), (me ^ 1, og_x), (me ^ 3, og_xc))
        grad = sum(
            lax.dot_general(
                lax.dynamic_index_in_dim(coords, i, 0, keepdims=False),
                og,
                (((0,), (0,)), ((), ())),
                preferred_element_type=f32,
            )
            for i, og in blocks
        )
        grad = exchange(grad.reshape(zl, zh * depth, width).astype(bf16), "zl")
        grad = jnp.sum(grad.astype(f32), axis=0)
        grad = exchange(grad.reshape(zh, depth, width).astype(bf16), "zh")
        grad = jnp.sum(grad.astype(f32), axis=0)

        new_first = beta_one * first_moment + (1.0 - beta_one) * grad
        new_second = beta_two * second_moment + (1.0 - beta_two) * grad * grad
        correct_one = 1.0 - beta_one**adam_step
        correct_two = 1.0 - beta_two**adam_step
        update = (
            new_first / correct_one / (jnp.sqrt(new_second / correct_two) + eps_value)
        ).astype(bf16)

        full = jnp.stack([update[:, i * half : (i + 1) * half] for i in range(c)])
        full = jnp.broadcast_to(full[None], (zh,) + full.shape)
        full = exchange(full.reshape(zh * c, depth, half), ("zh", "c"))
        full = spread(full.reshape(zh * c * depth, half), ("xl", "zl"), xl * zl)
        delta = jnp.dot(rows, full.reshape(ranks, half), preferred_element_type=f32)

        weight = jnp.stack([jnp.where(core == 0, mine, theirs), jnp.where(core == 0, theirs, mine)])
        fresh = weight - step_size * delta.reshape(c, height, half)
        fresh = jnp.broadcast_to(fresh[None], (nf,) + fresh.shape)
        new_weight = exchange(fresh.reshape(nf * c, height, half), ("y", "xh", "c"))
        new_weight = jnp.concatenate([new_weight[i] for i in range(nf * c)], axis=1)
        return (new_weight, new_first, new_second)

    return body


def split(mesh):
    names = ("xl", "zh", "zl", "c", "y", "xh")
    return Mesh(mesh.devices.reshape(2, 8, 4, 2, 4, 2), names)


def run_on(fine):
    sizes = dict(fine.shape)
    in_specs = (P(DP, FS), P(), P(DP, FS), P(DP, FS), P(DP, FS), P(DP, FS))
    out_specs = (P(DP, None), P(DP, FS), P(DP, FS))
    return jax.shard_map(
        build(sizes), mesh=fine, in_specs=in_specs, out_specs=out_specs, check_vma=False
    )


def solution(mesh):
    return run_on(split(mesh))
```

```python
import jax
import jax.numpy as jnp
from jax import lax
from jax.sharding import Mesh, PartitionSpec as P

beta_one = 0.9
beta_two = 0.999
adam_step = 2
eps_value = 1e-08
step_size = 1.0
lift = 16.0

f32 = jnp.float32
bf16 = jnp.bfloat16
DP = ("xl", "zh", "zl", "c")
FS = ("y", "xh")


def swap(x, axis):
    return lax.ppermute(x, axis, [(0, 1), (1, 0)])


def exchange(x, axis):
    return lax.all_to_all(x, axis, 0, 0, tiled=False)


def spread(x, axis, n):
    return exchange(jnp.broadcast_to(x[None], (n,) + x.shape), axis)


def rank_order(sizes, total):
    xl, zh, zl, c = (sizes[a] for a in DP)
    depth = total // (xl * zh * zl * c)
    new = lax.broadcasted_iota(jnp.int32, (total, total), 1)
    j = new % depth
    rest = new // depth
    izh = rest % zh
    rest = rest // zh
    izl = rest % zl
    rest = rest // zl
    ixl = rest % xl
    ic = rest // xl
    old = (((ixl * zh + izh) * zl + izl) * c + ic) * depth + j
    return (lax.broadcasted_iota(jnp.int32, (total, total), 0) == old).astype(bf16)


def build(sizes):
    xl, zh, zl, c = (sizes[a] for a in DP)
    nf = sizes["y"] * sizes["xh"]

    def body(activations, proj_basis, out_grad, master_weight, first_moment, second_moment):
        tokens, feats = activations.shape
        ranks = proj_basis.shape[1]
        width = out_grad.shape[1]
        depth = first_moment.shape[0]
        height = master_weight.shape[0]
        order = rank_order(sizes, ranks)

        acts = exchange(activations.reshape(nf, tokens // nf, feats), FS)
        own = lax.dot_general(
            acts,
            proj_basis.reshape(nf, feats, ranks),
            (((0, 2), (0, 1)), ((), ())),
            preferred_element_type=f32,
        ).astype(bf16)
        own = jnp.dot(own, order, preferred_element_type=f32).astype(bf16)
        own = own.reshape(tokens // nf, c * xl, ranks // (c * xl)).swapaxes(0, 1)
        own = jnp.broadcast_to(own[:, None], (c * xl, nf) + own.shape[1:])
        own = own.reshape((c * xl * nf,) + own.shape[2:])
        coords = exchange(own, ("c", "xl", "y", "xh"))
        coords = coords.reshape(c * xl, tokens, ranks // (c * xl))

        me = lax.axis_index("c") * xl + lax.axis_index("xl")
        og_x = swap(out_grad, "xl")
        og_c = swap(out_grad, "c")
        og_xc = swap(og_x, "c")
        blocks = ((me, out_grad), (me ^ 2, og_c), (me ^ 1, og_x), (me ^ 3, og_xc))
        grad = sum(
            lax.dot_general(
                lax.dynamic_index_in_dim(coords, i, 0, keepdims=False),
                og,
                (((0,), (0,)), ((), ())),
                preferred_element_type=f32,
            )
            for i, og in blocks
        )
        grad = exchange(grad.reshape(zl, zh * depth, width).astype(bf16), "zl")
        grad = jnp.sum(grad.astype(f32), axis=0)
        grad = exchange(grad.reshape(zh, depth, width).astype(bf16), "zh")
        grad = jnp.sum(grad.astype(f32), axis=0)

        new_first = beta_one * first_moment + (1.0 - beta_one) * grad
        new_second = beta_two * second_moment + (1.0 - beta_two) * grad * grad
        correct_one = 1.0 - beta_one**adam_step
        correct_two = 1.0 - beta_two**adam_step
        update = (
            new_first / correct_one / (jnp.sqrt(new_second / correct_two) + eps_value)
        ).astype(bf16)

        full = spread(update, "zh", zh).reshape(zh * depth, width)
        full = spread(full, ("xl", "zl"), xl * zl).reshape(ranks // c, width)
        other = swap(full, "c")

        basis_rows = lax.dynamic_slice_in_dim(proj_basis, lax.axis_index(DP) * height, height, 0)
        basis_rows = jnp.dot(basis_rows, order, preferred_element_type=f32).astype(bf16)
        basis_rows = basis_rows.reshape(height, c, ranks // c).swapaxes(0, 1)
        core = lax.axis_index("c")
        delta = jnp.dot(
            lax.dynamic_index_in_dim(basis_rows, core, 0, keepdims=False),
            full,
            preferred_element_type=f32,
        )
        delta = delta + jnp.dot(
            lax.dynamic_index_in_dim(basis_rows, 1 - core, 0, keepdims=False),
            other,
            preferred_element_type=f32,
        )
        fresh = master_weight - step_size * delta
        new_weight = spread((lift * fresh).astype(jnp.float16), FS, nf)
        new_weight = jnp.concatenate(
            [new_weight[i].astype(f32) * (1.0 / lift) for i in range(nf)], axis=1
        )
        return (new_weight, new_first, new_second)

    return body


def split(mesh):
    names = ("xl", "zh", "zl", "c", "y", "xh")
    return Mesh(mesh.devices.reshape(2, 8, 4, 2, 4, 2), names)


def run_on(fine):
    sizes = dict(fine.shape)
    in_specs = (P(DP, FS), P(), P(DP, FS), P(DP, FS), P(DP, FS), P(DP, FS))
    out_specs = (P(DP, None), P(DP, FS), P(DP, FS))
    return jax.shard_map(
        build(sizes), mesh=fine, in_specs=in_specs, out_specs=out_specs, check_vma=False
    )


def solution(mesh):
    return run_on(split(mesh))
```

```python
import jax
import jax.numpy as jnp
from jax import lax
from jax.sharding import Mesh, PartitionSpec as P

beta_one = 0.9
beta_two = 0.999
adam_step = 2
eps_value = 1e-08
step_size = 1.0
lift = 16.0

f32 = jnp.float32
bf16 = jnp.bfloat16
DP = ("xl", "zh", "zl", "c")
FS = ("y", "xh")


def swap(x, axis):
    return lax.ppermute(x, axis, [(0, 1), (1, 0)])


def exchange(x, axis):
    return lax.all_to_all(x, axis, 0, 0, tiled=False)


def spread(x, axis, n):
    return exchange(jnp.broadcast_to(x[None], (n,) + x.shape), axis)


def rank_order(sizes, total):
    xl, zh, zl, c = (sizes[a] for a in DP)
    depth = total // (xl * zh * zl * c)
    new = lax.broadcasted_iota(jnp.int32, (total, total), 1)
    j = new % depth
    rest = new // depth
    izh = rest % zh
    rest = rest // zh
    izl = rest % zl
    rest = rest // zl
    ixl = rest % xl
    ic = rest // xl
    old = (((ixl * zh + izh) * zl + izl) * c + ic) * depth + j
    return (lax.broadcasted_iota(jnp.int32, (total, total), 0) == old).astype(bf16)


def back_order(sizes, total):
    zh, zl, c = (sizes[a] for a in ("zh", "zl", "c"))
    depth = total // (zh * zl * c)
    new = lax.broadcasted_iota(jnp.int32, (total, total), 1)
    rest = new // depth
    izh = rest % zh
    rest = rest // zh
    old = ((izh * zl + rest % zl) * c + rest // zl) * depth + new % depth
    return (lax.broadcasted_iota(jnp.int32, (total, total), 0) == old).astype(bf16)


def build(sizes):
    xl, zh, zl, c = (sizes[a] for a in DP)
    nf = sizes["y"] * sizes["xh"]

    def body(activations, proj_basis, out_grad, master_weight, first_moment, second_moment):
        tokens, feats = activations.shape
        ranks = proj_basis.shape[1]
        width = out_grad.shape[1]
        depth = first_moment.shape[0]
        height = master_weight.shape[0]
        order = rank_order(sizes, ranks)

        acts = exchange(activations.reshape(nf, tokens // nf, feats), FS)

        block = ranks // xl
        back = back_order(sizes, block)
        rows = lax.dynamic_slice_in_dim(proj_basis, lax.axis_index(DP) * height, height, 0)
        rows = jnp.concatenate(
            [
                jnp.dot(
                    rows[:, i * block : (i + 1) * block], back, preferred_element_type=f32
                ).astype(bf16)
                for i in range(xl)
            ],
            axis=1,
        )
        acts, rows = lax.optimization_barrier((acts, rows))
        own = lax.dot_general(
            acts,
            proj_basis.reshape(nf, feats, ranks),
            (((0, 2), (0, 1)), ((), ())),
            preferred_element_type=f32,
        ).astype(bf16)
        own = jnp.dot(own, order, preferred_element_type=f32).astype(bf16)
        own = own.reshape(tokens // nf, c * xl, ranks // (c * xl)).swapaxes(0, 1)
        own = jnp.broadcast_to(own[:, None], (c * xl, nf) + own.shape[1:])
        own = own.reshape((c * xl * nf,) + own.shape[2:])
        coords = exchange(own, ("c", "xl", "y", "xh"))
        coords = coords.reshape(c * xl, tokens, ranks // (c * xl))

        me = lax.axis_index("c") * xl + lax.axis_index("xl")
        og_x = swap(out_grad, "xl")
        og_c = swap(out_grad, "c")
        og_xc = swap(og_x, "c")
        blocks = ((me, out_grad), (me ^ 2, og_c), (me ^ 1, og_x), (me ^ 3, og_xc))
        grad = sum(
            lax.dot_general(
                lax.dynamic_index_in_dim(coords, i, 0, keepdims=False),
                og,
                (((0,), (0,)), ((), ())),
                preferred_element_type=f32,
            )
            for i, og in blocks
        )
        grad = exchange(grad.reshape(zl, zh * depth, width).astype(bf16), "zl")
        grad = jnp.sum(grad.astype(f32), axis=0)
        grad = exchange(grad.reshape(zh, depth, width).astype(bf16), "zh")
        grad = jnp.sum(grad.astype(f32), axis=0)

        new_first = beta_one * first_moment + (1.0 - beta_one) * grad
        new_second = beta_two * second_moment + (1.0 - beta_two) * grad * grad
        correct_one = 1.0 - beta_one**adam_step
        correct_two = 1.0 - beta_two**adam_step
        update = (
            new_first / correct_one / (jnp.sqrt(new_second / correct_two) + eps_value)
        ).astype(bf16)

        full = spread(update, "zh", zh).reshape(zh * depth, width)
        full = spread(full, "zl", zl).reshape(zl * zh * depth, width)
        full = lax.all_gather(full, ("xl", "c"), axis=0, tiled=True)
        delta = jnp.dot(rows, full, preferred_element_type=f32)
        fresh = master_weight - step_size * delta
        new_weight = spread((lift * fresh).astype(jnp.float16), FS, nf)
        new_weight = jnp.concatenate(
            [new_weight[i].astype(f32) * (1.0 / lift) for i in range(nf)], axis=1
        )
        return (new_weight, new_first, new_second)

    return body


def split(mesh):
    names = ("xl", "zh", "zl", "c", "y", "xh")
    return Mesh(mesh.devices.reshape(2, 8, 4, 2, 4, 2), names)


def run_on(fine):
    sizes = dict(fine.shape)
    in_specs = (P(DP, FS), P(), P(DP, FS), P(DP, FS), P(DP, FS), P(DP, FS))
    out_specs = (P(DP, None), P(DP, FS), P(DP, FS))
    return jax.shard_map(
        build(sizes), mesh=fine, in_specs=in_specs, out_specs=out_specs, check_vma=False
    )


def solution(mesh):
    return run_on(split(mesh))
```

```python
import jax
import jax.numpy as jnp
from jax import lax
from jax.sharding import Mesh, PartitionSpec as P

beta_one = 0.9
beta_two = 0.999
adam_step = 2
eps_value = 1e-08
step_size = 1.0
lift = 16.0

f32 = jnp.float32
bf16 = jnp.bfloat16
DP = ("xl", "zh", "zl", "c")
FS = ("y", "xh")


def swap(x, axis):
    return lax.ppermute(x, axis, [(0, 1), (1, 0)])


def exchange(x, axis):
    return lax.all_to_all(x, axis, 0, 0, tiled=False)


def spread(x, axis, n):
    return exchange(jnp.broadcast_to(x[None], (n,) + x.shape), axis)


def rank_order(sizes, total):
    xl, zh, zl, c = (sizes[a] for a in DP)
    depth = total // (xl * zh * zl * c)
    new = lax.broadcasted_iota(jnp.int32, (total, total), 1)
    j = new % depth
    rest = new // depth
    izh = rest % zh
    rest = rest // zh
    izl = rest % zl
    rest = rest // zl
    ixl = rest % xl
    ic = rest // xl
    old = (((ixl * zh + izh) * zl + izl) * c + ic) * depth + j
    return (lax.broadcasted_iota(jnp.int32, (total, total), 0) == old).astype(bf16)


def back_order(sizes, total):
    zh, zl, c = (sizes[a] for a in ("zh", "zl", "c"))
    depth = total // (zh * zl * c)
    new = lax.broadcasted_iota(jnp.int32, (total, total), 1)
    rest = new // depth
    izh = rest % zh
    rest = rest // zh
    old = ((izh * zl + rest % zl) * c + rest // zl) * depth + new % depth
    return (lax.broadcasted_iota(jnp.int32, (total, total), 0) == old).astype(bf16)


def build(sizes):
    xl, zh, zl, c = (sizes[a] for a in DP)
    nf = sizes["y"] * sizes["xh"]

    def body(activations, proj_basis, out_grad, master_weight, first_moment, second_moment):
        tokens, feats = activations.shape
        ranks = proj_basis.shape[1]
        width = out_grad.shape[1]
        depth = first_moment.shape[0]
        height = master_weight.shape[0]
        order = rank_order(sizes, ranks)

        acts = exchange(activations.reshape(nf, tokens // nf, feats), FS)

        block = ranks // xl
        back = back_order(sizes, block)
        rows = lax.dynamic_slice_in_dim(proj_basis, lax.axis_index(DP) * height, height, 0)
        rows = jnp.concatenate(
            [
                jnp.dot(
                    rows[:, i * block : (i + 1) * block], back, preferred_element_type=f32
                ).astype(bf16)
                for i in range(xl)
            ],
            axis=1,
        )
        acts, rows, order = lax.optimization_barrier((acts, rows, order))
        own = lax.dot_general(
            acts,
            proj_basis.reshape(nf, feats, ranks),
            (((0, 2), (0, 1)), ((), ())),
            preferred_element_type=f32,
        ).astype(bf16)
        own = jnp.dot(own, order, preferred_element_type=f32).astype(bf16)
        own = own.reshape(tokens // nf, c * xl, ranks // (c * xl)).swapaxes(0, 1)
        own = jnp.broadcast_to(own[:, None], (c * xl, nf) + own.shape[1:])
        own = own.reshape((c * xl * nf,) + own.shape[2:])
        coords = exchange(own, ("c", "xl", "y", "xh"))
        coords = coords.reshape(c * xl, tokens, ranks // (c * xl))

        me = lax.axis_index("c") * xl + lax.axis_index("xl")
        og_x = swap(out_grad, "xl")
        og_c = swap(out_grad, "c")
        og_xc = swap(og_x, "c")
        blocks = ((me, out_grad), (me ^ 2, og_c), (me ^ 1, og_x), (me ^ 3, og_xc))
        grad = sum(
            lax.dot_general(
                lax.dynamic_index_in_dim(coords, i, 0, keepdims=False),
                og,
                (((0,), (0,)), ((), ())),
                preferred_element_type=f32,
            )
            for i, og in blocks
        )
        grad = exchange(grad.reshape(zl, zh * depth, width).astype(bf16), "zl")
        grad = jnp.sum(grad.astype(f32), axis=0)
        grad = exchange(grad.reshape(zh, depth, width).astype(bf16), "zh")
        grad = jnp.sum(grad.astype(f32), axis=0)

        new_first = beta_one * first_moment + (1.0 - beta_one) * grad
        new_second = beta_two * second_moment + (1.0 - beta_two) * grad * grad
        correct_one = 1.0 - beta_one**adam_step
        correct_two = 1.0 - beta_two**adam_step
        update = (
            new_first / correct_one / (jnp.sqrt(new_second / correct_two) + eps_value)
        ).astype(bf16)

        full = spread(update, "zh", zh).reshape(zh * depth, width)
        full = spread(full, "zl", zl).reshape(zl * zh * depth, width)
        full = lax.all_gather(full, ("xl", "c"), axis=0, tiled=True)
        delta = jnp.dot(rows, full, preferred_element_type=f32)
        fresh = master_weight - step_size * delta
        new_weight = spread((lift * fresh).astype(jnp.float16), FS, nf)
        new_weight = jnp.concatenate(
            [new_weight[i].astype(f32) * (1.0 / lift) for i in range(nf)], axis=1
        )
        return (new_weight, new_first, new_second)

    return body


def split(mesh):
    names = ("xl", "zh", "zl", "c", "y", "xh")
    return Mesh(mesh.devices.reshape(2, 8, 4, 2, 4, 2), names)


def run_on(fine):
    sizes = dict(fine.shape)
    in_specs = (P(DP, FS), P(), P(DP, FS), P(DP, FS), P(DP, FS), P(DP, FS))
    out_specs = (P(DP, None), P(DP, FS), P(DP, FS))
    return jax.shard_map(
        build(sizes), mesh=fine, in_specs=in_specs, out_specs=out_specs, check_vma=False
    )


def solution(mesh):
    return run_on(split(mesh))
```

```python
import jax
import jax.numpy as jnp
from jax import lax
from jax.sharding import Mesh, PartitionSpec as P

beta_one = 0.9
beta_two = 0.999
adam_step = 2
eps_value = 1e-08
step_size = 1.0
lift = 16.0

f32 = jnp.float32
bf16 = jnp.bfloat16
DP = ("xl", "zh", "zl", "c")
FS = ("y", "xh")


def swap(x, axis):
    return lax.ppermute(x, axis, [(0, 1), (1, 0)])


def exchange(x, axis):
    return lax.all_to_all(x, axis, 0, 0, tiled=False)


def spread(x, axis, n):
    return exchange(jnp.broadcast_to(x[None], (n,) + x.shape), axis)


def rank_order(sizes, total):
    xl, zh, zl, c = (sizes[a] for a in DP)
    depth = total // (xl * zh * zl * c)
    new = lax.broadcasted_iota(jnp.int32, (total, total), 1)
    j = new % depth
    rest = new // depth
    izh = rest % zh
    rest = rest // zh
    izl = rest % zl
    rest = rest // zl
    ixl = rest % xl
    ic = rest // xl
    old = (((ixl * zh + izh) * zl + izl) * c + ic) * depth + j
    return (lax.broadcasted_iota(jnp.int32, (total, total), 0) == old).astype(bf16)


def back_order(sizes, total):
    zh, zl, c = (sizes[a] for a in ("zh", "zl", "c"))
    depth = total // (zh * zl * c)
    new = lax.broadcasted_iota(jnp.int32, (total, total), 1)
    rest = new // depth
    izh = rest % zh
    rest = rest // zh
    old = ((izh * zl + rest % zl) * c + rest // zl) * depth + new % depth
    return (lax.broadcasted_iota(jnp.int32, (total, total), 0) == old).astype(bf16)


def build(sizes):
    xl, zh, zl, c = (sizes[a] for a in DP)
    nf = sizes["y"] * sizes["xh"]

    def body(activations, proj_basis, out_grad, master_weight, first_moment, second_moment):
        tokens, feats = activations.shape
        ranks = proj_basis.shape[1]
        width = out_grad.shape[1]
        depth = first_moment.shape[0]
        height = master_weight.shape[0]
        order = rank_order(sizes, ranks)

        acts = exchange(activations.reshape(nf, tokens // nf, feats), FS)

        block = ranks // xl
        back = back_order(sizes, block)
        rows = lax.dynamic_slice_in_dim(proj_basis, lax.axis_index(DP) * height, height, 0)
        rows = jnp.concatenate(
            [
                jnp.dot(
                    rows[:, i * block : (i + 1) * block], back, preferred_element_type=f32
                ).astype(bf16)
                for i in range(xl)
            ],
            axis=1,
        )
        acts, rows = lax.optimization_barrier((acts, rows))
        own = lax.dot_general(
            acts,
            proj_basis.reshape(nf, feats, ranks),
            (((0, 2), (0, 1)), ((), ())),
            preferred_element_type=f32,
        ).astype(bf16)
        own = jnp.dot(own, order, preferred_element_type=f32).astype(bf16)
        own = own.reshape(tokens // nf, c * xl, ranks // (c * xl)).swapaxes(0, 1)
        own = jnp.broadcast_to(own[:, None], (c * xl, nf) + own.shape[1:])
        own = own.reshape((c * xl * nf,) + own.shape[2:])
        coords = exchange(own, ("c", "xl", "y", "xh"))
        coords = coords.reshape(c * xl, tokens, ranks // (c * xl))

        me = lax.axis_index("c") * xl + lax.axis_index("xl")
        og_x = swap(out_grad, "xl")
        og_c = swap(out_grad, "c")
        og_xc = swap(og_c, "xl")
        blocks = ((me, out_grad), (me ^ 2, og_c), (me ^ 1, og_x), (me ^ 3, og_xc))
        grad = sum(
            lax.dot_general(
                lax.dynamic_index_in_dim(coords, i, 0, keepdims=False),
                og,
                (((0,), (0,)), ((), ())),
                preferred_element_type=f32,
            )
            for i, og in blocks
        )
        grad = exchange(grad.reshape(zl, zh * depth, width).astype(bf16), "zl")
        grad = jnp.sum(grad.astype(f32), axis=0)
        grad = exchange(grad.reshape(zh, depth, width).astype(bf16), "zh")
        grad = jnp.sum(grad.astype(f32), axis=0)

        new_first = beta_one * first_moment + (1.0 - beta_one) * grad
        new_second = beta_two * second_moment + (1.0 - beta_two) * grad * grad
        correct_one = 1.0 - beta_one**adam_step
        correct_two = 1.0 - beta_two**adam_step
        update = (
            new_first / correct_one / (jnp.sqrt(new_second / correct_two) + eps_value)
        ).astype(bf16)

        full = spread(update, "zh", zh).reshape(zh * depth, width)
        full = spread(full, "zl", zl).reshape(zl * zh * depth, width)
        full = lax.all_gather(full, ("xl", "c"), axis=0, tiled=True)
        delta = jnp.dot(rows, full, preferred_element_type=f32)
        fresh = master_weight - step_size * delta
        new_weight = spread((lift * fresh).astype(jnp.float16), FS, nf)
        new_weight = jnp.concatenate(
            [new_weight[i].astype(f32) * (1.0 / lift) for i in range(nf)], axis=1
        )
        return (new_weight, new_first, new_second)

    return body


def split(mesh):
    names = ("xl", "zh", "zl", "c", "y", "xh")
    return Mesh(mesh.devices.reshape(2, 8, 4, 2, 4, 2), names)


def run_on(fine):
    sizes = dict(fine.shape)
    in_specs = (P(DP, FS), P(), P(DP, FS), P(DP, FS), P(DP, FS), P(DP, FS))
    out_specs = (P(DP, None), P(DP, FS), P(DP, FS))
    return jax.shard_map(
        build(sizes), mesh=fine, in_specs=in_specs, out_specs=out_specs, check_vma=False
    )


def solution(mesh):
    return run_on(split(mesh))
```
